1024 devices in a mesh: ctx: 128 (over x, z), head: 8 (over y, core).
Axes of the slice: x: 4, y: 4, z: 32, core: 2. Of those that a mesh axis runs over, the one named last changes fastest.
Arguments:
- queries: bfloat16 [16384, 12288], P('ctx', 'head'), may hold values from -6 to 6, as said below
- keys: bfloat16 [16384, 1024], P('ctx', 'head'), may hold values from -6 to 6
- values: bfloat16 [16384, 1024], P('ctx', 'head'), may hold values from -6 to 6
- out_grad: bfloat16 [16384, 12288], P('ctx', 'head'), may hold values from -45 to 45
- doc_lengths: int32 [32], replicated, may hold values from 1 to 1024, 16384 in all
Outputs:
- grad_queries: bfloat16 [16384, 12288], P('ctx', 'head')
- grad_keys: bfloat16 [16384, 1024], P('ctx', 'head')
- grad_values: bfloat16 [16384, 1024], P('ctx', 'head')
- grad_rms: float32 [], replicated
The draws below stay inside these ranges and needn't reach their ends.
Inputs may be any that keep to these rules, and one draw needn't show every extreme that they name: `queries`: query and key entries lie within the stated range. `doc_lengths`: the lengths sum to 16384; the longest is exactly 1024.
All inputs are finite; a program needn't handle non-finite values.
Results may differ from the reference program's by a relative error of at most 0.0084.
Values may be sent and summed in bfloat16 or wider, within the bound.
A program may use at most 32 MiB of HBM per device.

```python
import math
import jax
import jax.numpy as jnp
import numpy as np
from jax import lax

QH = 96
KVH = 8
HD = 128
TOK_DEV = 128
SPAN = 8
MOST = 1024
TOKENS = 16384
NDOCS = 32
N_CTX = 128


def draw_queries(key, part):
    key = jax.random.fold_in(key, 11)
    base = jnp.clip(jax.random.normal(key, (TOKENS, QH * HD), jnp.float32), -6.0, 6.0)
    return base.astype(jnp.bfloat16)


def draw_keys(key, part):
    key = jax.random.fold_in(key, 23)
    base = jnp.clip(jax.random.normal(key, (TOKENS, KVH * HD), jnp.float32), -6.0, 6.0)
    return base.astype(jnp.bfloat16)


def draw_out_grad(key, part):
    key = jax.random.fold_in(key, 37)
    noise_key, bias_key = jax.random.split(key)
    fraction = jnp.arange(TOKENS, dtype=jnp.float32)[:, None] / TOKENS
    column_bias = jnp.clip(jax.random.normal(bias_key, (1, QH * HD), jnp.float32), -3.0, 3.0)
    noise = jnp.clip(jax.random.normal(noise_key, (TOKENS, QH * HD), jnp.float32), -4.0, 4.0)
    level = 0.4 * jnp.exp(fraction * math.log(16.0))
    return (level * (noise + column_bias)).astype(jnp.bfloat16)


def shard_levels(key, extent, cuts, smallest, high):
    loudness, own = 1.0, jax.random.fold_in(key, 6)
    for axis_at, shards_of in cuts:
        heights = jnp.exp(jax.random.uniform(jax.random.fold_in(own, axis_at), (shards_of,), jnp.float32, smallest / len(cuts), high / len(cuts)))
        loudness = loudness * jnp.repeat(heights, extent[axis_at] // shards_of).reshape([-1 if axis == axis_at else 1 for axis in range(len(extent))])
    return loudness


def length_profile(count, total, limit, lean):
    loads = [(1 << 20) // math.isqrt(grade ** lean) + 1 for grade in range(2, count + 1)]
    rest, given = total - limit - (count - 1), [1] * (count - 1)
    while rest > 0:
        free = [i for i in range(count - 1) if given[i] < limit]
        whole, left = sum([loads[i] for i in free]), rest
        for i in free:
            more = min(limit - given[i], max(1, left * loads[i] // whole), rest)
            given[i] = given[i] + more
            rest = rest - more
    return np.array([limit] + given)


def uneven_parts(stream_key, number_of, total, bound, slope):
    if number_of == 2:
        one = jax.random.randint(stream_key, (), max(1, total - bound), min(bound, total - 1) + 1)
        return jnp.stack([one, total - one])
    sizes = jnp.asarray(length_profile(number_of, total, bound, slope), jnp.int32)
    twos = (number_of - 1) // 2
    donor, receiver = sizes[1:1 + 2 * twos:2], sizes[2:2 + 2 * twos:2]
    room = jnp.minimum(donor - 1, bound - receiver)
    moved = jax.random.randint(jax.random.fold_in(stream_key, 1), (twos,), 0, 1 << 20) % (room + 1)
    sizes = sizes.at[1:1 + 2 * twos:2].set(donor - moved).at[2:2 + 2 * twos:2].set(receiver + moved)
    return sizes[jax.random.permutation(jax.random.fold_in(stream_key, 2), number_of)]


def scatter_about(rng, shape, spread, limit, cuts=(), kind=jnp.bfloat16):
    entries = spread * jax.random.normal(rng, shape, jnp.float32)
    if cuts:
        entries = entries * shard_levels(rng, shape, cuts, -0.22, 0.18)
    return jnp.clip(entries, -limit, limit).astype(kind)


def setup_inputs(seed: int = 0) -> dict:
    streams_of = jax.random.split(jax.random.key(seed), 6)
    queries = draw_queries(jax.random.fold_in(streams_of[5], 71), 0)
    keys = draw_keys(jax.random.fold_in(streams_of[5], 71), 0)
    values = scatter_about(streams_of[2], (TOKENS, KVH * HD), 1.0, 6.0, ((0, 128), (1, 8)))
    out_grad = draw_out_grad(jax.random.fold_in(streams_of[5], 71), 0)
    doc_lengths = uneven_parts(streams_of[4], NDOCS, TOKENS, MOST, 2).astype(jnp.int32)
    return {"queries": queries, "keys": keys, "values": values, "out_grad": out_grad, "doc_lengths": doc_lengths}


def token_starts(doc_lengths, positions):
    lengths = doc_lengths.astype(jnp.int32)
    starts = (jnp.cumsum(lengths, dtype=jnp.int32) - lengths).astype(jnp.int32)
    before = starts[None, :] <= positions[:, None]
    return lax.optimization_barrier(jnp.max(jnp.where(before, starts[None, :], 0), axis=1)).astype(jnp.int32)

def reference(queries, keys, values, out_grad, doc_lengths):
    group_size = QH // KVH
    score_scale = HD ** (-0.5)
    window = (SPAN + 1) * TOK_DEV
    margin = SPAN * TOK_DEV
    positions = jnp.arange(TOKENS, dtype=jnp.int32)
    first_allowed = token_starts(doc_lengths, positions)
    keys_padded = jnp.pad(keys, ((margin, 0), (0, 0))).reshape(TOKENS + margin, KVH, HD)
    values_padded = jnp.pad(values, ((margin, 0), (0, 0))).reshape(TOKENS + margin, KVH, HD)
    query_heads = queries.reshape(TOKENS, KVH, group_size, HD)
    grad_heads = out_grad.reshape(TOKENS, KVH, group_size, HD)

    def block(carry, block_no):
        dk_acc, dv_acc = carry
        begin = (block_no * TOK_DEV).astype(jnp.int32)
        query_part = lax.dynamic_slice_in_dim(query_heads, begin, TOK_DEV, 0).astype(jnp.float32)
        grad_part = lax.dynamic_slice_in_dim(grad_heads, begin, TOK_DEV, 0).astype(jnp.float32)
        keys_part = lax.dynamic_slice_in_dim(keys_padded, begin, window, 0).astype(jnp.float32)
        values_part = lax.dynamic_slice_in_dim(values_padded, begin, window, 0).astype(jnp.float32)
        query_pos = begin + jnp.arange(TOK_DEV, dtype=jnp.int32)
        key_pos = begin - margin + jnp.arange(window, dtype=jnp.int32)
        starts_part = lax.dynamic_slice_in_dim(first_allowed, begin, TOK_DEV, 0)
        allowed = (key_pos[None, :] >= starts_part[:, None]) & (key_pos[None, :] <= query_pos[:, None])
        scores = jnp.einsum('qjgd,kjd->jgqk', query_part, keys_part) * score_scale
        scores = jnp.where(allowed[None, None], scores, -jnp.inf)
        peak = lax.optimization_barrier(jnp.max(scores, axis=3, keepdims=True))
        log_total = peak + jnp.log(lax.optimization_barrier(jnp.sum(jnp.exp(scores - peak), axis=3, keepdims=True)))
        weights = jnp.where(allowed[None, None], jnp.exp(scores - log_total), 0.0)
        weights_low = weights.astype(jnp.bfloat16).astype(jnp.float32)
        attended = jnp.einsum('jgqk,kjd->qjgd', weights_low, values_part)
        row_dots = lax.optimization_barrier(jnp.sum(grad_part * attended, axis=3))
        grad_weights = jnp.einsum('qjgd,kjd->jgqk', grad_part, values_part)
        grad_scores = weights * (grad_weights - jnp.transpose(row_dots, (1, 2, 0))[..., None])
        grad_scores = grad_scores.astype(jnp.bfloat16).astype(jnp.float32)
        grad_query = jnp.einsum('jgqk,kjd->qjgd', grad_scores, keys_part) * score_scale
        grad_key = jnp.einsum('jgqk,qjgd->kjd', grad_scores, query_part) * score_scale
        grad_value = jnp.einsum('jgqk,qjgd->kjd', weights_low, grad_part)
        dk_acc = lax.dynamic_update_slice_in_dim(dk_acc, lax.dynamic_slice_in_dim(dk_acc, begin, window, 0) + grad_key.reshape(window, KVH * HD), begin, 0)
        dv_acc = lax.dynamic_update_slice_in_dim(dv_acc, lax.dynamic_slice_in_dim(dv_acc, begin, window, 0) + grad_value.reshape(window, KVH * HD), begin, 0)
        return ((dk_acc, dv_acc), grad_query.reshape(TOK_DEV, QH * HD))
    zeros = jnp.zeros((TOKENS + margin, KVH * HD), jnp.float32)
    (dk_acc, dv_acc), blocks = lax.scan(block, (zeros, zeros), jnp.arange(N_CTX, dtype=jnp.int32))
    grad_queries = blocks.reshape(TOKENS, QH * HD)
    grad_keys = dk_acc[margin:]
    grad_values = dv_acc[margin:]
    total = jnp.sum(grad_queries * grad_queries) + jnp.sum(grad_keys * grad_keys) + jnp.sum(grad_values * grad_values)
    grad_rms = jnp.sqrt(total / (TOKENS * (QH * HD + 2 * KVH * HD)))
    return (grad_queries.astype(jnp.bfloat16), grad_keys.astype(jnp.bfloat16), grad_values.astype(jnp.bfloat16), grad_rms)
```

```python
from functools import partial
import math

import jax
import jax.numpy as jnp
from jax import lax
from jax.experimental import pallas as pl
from jax.experimental.pallas import tpu as pltpu
from jax.sharding import PartitionSpec as P

HD = 128
LOG2E = 1.4426950408889634
MASKED = -1e30
MESH = pl.DeviceIdType.MESH
F32 = jnp.float32
BF16 = jnp.bfloat16
PIECE = 128


def nn(a, b):
    return lax.dot_general(a, b, (((1,), (0,)), ((), ())), preferred_element_type=F32)


def kernel(
    sizes, scale, count_all,
    doc_ref, q_ref, k_ref, v_ref, do_ref,
    dq_ref, dk_ref, dv_ref, rms_ref,
    kv, kt, qt, dot_, qs, dos, p_buf, dp_buf, ds_buf, pb_buf, dqt,
    m_all, l_row, r_row, g_out, g_in,
    sum_head, sum_lo, sum_hi,
    kv_send, kv_recv, g_send, g_recv, s_send, s_recv,
):
    n_ctx, n_head, n_lo, reach, docs = sizes
    n_hi = n_ctx // n_lo
    tok = q_ref.shape[0]
    heads = q_ref.shape[1] // HD
    wide = heads * tok
    pieces = 2 * tok // PIECE
    me = lax.axis_index("ctx")
    mh = lax.axis_index("head")
    right = lax.rem(me + 1, n_ctx)
    left = lax.rem(me + n_ctx - 1, n_ctx)
    my_lo = lax.rem(me, n_lo)
    my_hi = lax.div(me, n_lo)

    def head_partner(i):
        return {"head": lax.rem(mh + i, n_head)}

    def lo_partner(i):
        return {"ctx": my_hi * n_lo + lax.rem(my_lo + i, n_lo)}

    def hi_partner(i):
        return {"ctx": lax.rem(my_hi + i, n_hi) * n_lo + my_lo}

    barrier = pltpu.get_barrier_semaphore()
    pl.semaphore_signal(barrier, inc=1, device_id={"ctx": right}, device_id_type=MESH)
    pl.semaphore_signal(barrier, inc=1, device_id={"ctx": left}, device_id_type=MESH)
    for partner, n in ((head_partner, n_head), (lo_partner, n_lo), (hi_partner, n_hi)):

        def greet(i, carry, partner=partner):
            pl.semaphore_signal(barrier, inc=1, device_id=partner(i), device_id_type=MESH)
            return carry

        lax.fori_loop(1, n, greet, 0)

    kv[0, 0:tok, :] = k_ref[...]
    kv[0, tok : 2 * tok, :] = v_ref[...]
    for h in range(heads):
        cols = slice(h * HD, (h + 1) * HD)
        rows = slice(h * tok, (h + 1) * tok)
        qs[rows, :] = q_ref[:, cols]
        dos[rows, :] = do_ref[:, cols]
        qt[:, rows] = q_ref[:, cols].T
        dot_[:, rows] = do_ref[:, cols].T

    pos = me * tok + lax.broadcasted_iota(jnp.int32, (8, tok), 1)
    first = jnp.zeros((8, tok), jnp.int32)
    begin = jnp.int32(0)
    for i in range(docs):
        first = jnp.where(begin <= pos, begin, first)
        begin = begin + doc_ref[i]
    first = first[0:1]
    pos = pos[0:1]

    pl.semaphore_wait(barrier, 2 + (n_head - 1) + (n_lo - 1) + (n_hi - 1))

    def kv_copy(d, i):
        rows = pl.ds(i * PIECE, PIECE)
        return pltpu.make_async_remote_copy(
            src_ref=kv.at[d, rows],
            dst_ref=kv.at[d + 1, rows],
            send_sem=kv_send.at[d, i],
            recv_sem=kv_recv.at[d, i],
            device_id={"ctx": right},
            device_id_type=MESH,
        )

    def g_copy(d, i):
        rows = pl.ds(i * PIECE, PIECE)
        return pltpu.make_async_remote_copy(
            src_ref=g_out.at[d, rows],
            dst_ref=g_in.at[d, rows],
            send_sem=g_send.at[d, i],
            recv_sem=g_recv.at[d, i],
            device_id={"ctx": left},
            device_id_type=MESH,
        )

    chunk = 256
    chunks = [slice(j, j + chunk) for j in range(0, wide, chunk)]

    def scores_of(d, opening):
        key = (me - d) * tok + lax.broadcasted_iota(jnp.int32, (tok, tok), 0)
        fine = (key >= first) & (key <= pos)
        bias = jnp.where(fine, 0.0, MASKED)
        bias = jnp.concatenate([bias] * (chunk // tok), axis=1)
        k_d = kv[d, 0:tok, :]
        v_d = kv[d, tok : 2 * tok, :]
        kt[d] = k_d.T
        for cols in chunks:
            s = nn(k_d, qt[:, cols]) * (scale * LOG2E) + bias
            top = jnp.max(s, axis=0, keepdims=True)
            if opening:
                m_new = top
            else:
                m_old = m_all[d - 1, :, cols]
                m_new = jnp.maximum(m_old, top)
            p = jnp.exp2(s - m_new)
            dp = nn(v_d, dot_[:, cols])
            p_buf[d, :, cols] = p
            dp_buf[d, :, cols] = dp
            l_add = jnp.sum(p, axis=0, keepdims=True)
            r_add = jnp.sum(p * dp, axis=0, keepdims=True)
            if not opening:
                shrink = jnp.exp2(m_old - m_new)
                l_add = l_add + shrink * l_row[:, cols]
                r_add = r_add + shrink * r_row[:, cols]
            m_all[d, :, cols] = m_new
            l_row[:, cols] = l_add
            r_row[:, cols] = r_add

    for i in range(pieces):
        kv_copy(0, i).start()
    scores_of(0, True)

    def gather_step(d, carry):
        for i in range(pieces):
            kv_copy(d - 1, i).wait_recv()

            @pl.when(d < reach)
            def _(i=i):
                kv_copy(d, i).start()

        scores_of(d, False)
        return carry

    lax.fori_loop(1, reach + 1, gather_step, 0)

    inverse = 1.0 / l_row[...]
    l_row[...] = inverse
    r_row[...] = r_row[...] * inverse

    def grads_of(d):
        for cols in chunks:
            factor = jnp.exp2(m_all[d, :, cols] - m_all[reach, :, cols]) * l_row[:, cols]
            w = p_buf[d, :, cols] * factor
            pb_buf[:, cols] = w.astype(BF16)
            ds_buf[:, cols] = (w * (dp_buf[d, :, cols] - r_row[:, cols])).astype(BF16)
        dk = nn(ds_buf[...], qs[...]) * scale
        dv = nn(pb_buf[...], dos[...])
        return dk, dv

    def queries_of(d, opening):
        for cols in chunks:
            part = nn(kt[d], ds_buf[:, cols])
            if opening:
                dqt[:, cols] = part
            else:
                dqt[:, cols] = dqt[:, cols] + part

    def send_back(d):
        for i in range(pieces):
            g_copy(d, i).start()

    dk, dv = grads_of(reach)
    g_out[reach, 0:tok, :] = dk.astype(BF16)
    g_out[reach, tok : 2 * tok, :] = dv.astype(BF16)
    send_back(reach)
    queries_of(reach, True)

    def return_step(step, carry):
        d = reach - step
        dk, dv = grads_of(d)
        for i in range(pieces):
            g_copy(d + 1, i).wait_recv()
        g_out[d, 0:tok, :] = (dk + g_in[d + 1, 0:tok, :].astype(F32)).astype(BF16)
        g_out[d, tok : 2 * tok, :] = (dv + g_in[d + 1, tok : 2 * tok, :].astype(F32)).astype(BF16)
        send_back(d)
        queries_of(d, False)
        return carry

    lax.fori_loop(1, reach, return_step, 0)
    dk, dv = grads_of(0)
    queries_of(0, False)
    squares = jnp.zeros((8, HD), F32)
    for h in range(heads):
        part = dqt[:, h * tok : (h + 1) * tok] * scale
        squares = squares + jnp.sum((part * part).reshape(HD // 8, 8, tok), axis=0)
        dq_ref[:, h * HD : (h + 1) * HD] = part.T.astype(BF16)
    for i in range(pieces):
        g_copy(1, i).wait_recv()
    dk = dk + g_in[1, 0:tok, :].astype(F32)
    dv = dv + g_in[1, tok : 2 * tok, :].astype(F32)
    both = dk * dk + dv * dv
    squares = squares + jnp.sum(both.reshape(tok // 8, 8, HD), axis=0)

    sends = 0
    for level, (partner, n, mine, slots) in enumerate((
        (head_partner, n_head, mh, sum_head),
        (lo_partner, n_lo, my_lo, sum_lo),
        (hi_partner, n_hi, my_hi, sum_hi),
    )):
        slots[mine] = squares

        def push(i, carry, partner=partner, mine=mine, slots=slots, level=level):
            pltpu.make_async_remote_copy(
                src_ref=slots.at[mine],
                dst_ref=slots.at[mine],
                send_sem=s_send.at[level],
                recv_sem=s_recv.at[level],
                device_id=partner(i),
                device_id_type=MESH,
            ).start()
            return carry

        lax.fori_loop(1, n, push, 0)
        if level == 0:
            dk_ref[...] = dk.astype(BF16)
            dv_ref[...] = dv.astype(BF16)
        if n == 1:
            continue
        others = slots.at[pl.ds(0, n - 1)]
        pltpu.make_async_copy(others, others, s_recv.at[level]).wait()
        squares = slots[0]
        for i in range(1, n):
            squares = squares + slots[i]
    rms_ref[...] = jnp.broadcast_to(jnp.sqrt(jnp.sum(squares) / count_all), rms_ref.shape)

    for level, (n, slots) in enumerate(((n_head, sum_head), (n_lo, sum_lo), (n_hi, sum_hi))):
        if n == 1:
            continue
        others = slots.at[pl.ds(0, n - 1)]
        pltpu.make_async_copy(others, others, s_send.at[level]).wait()
    for d in range(reach):
        for i in range(pieces):
            kv_copy(d, i).wait_send()
            g_copy(d + 1, i).wait_send()


def local(mesh_sizes, queries, keys, values, out_grad, doc_lengths):
    n_ctx, n_head = mesh_sizes
    tok, q_cols = queries.shape
    wide = q_cols // HD * tok
    n_lo = min(8, n_ctx)
    reach = min(8, n_ctx // 2)
    docs = doc_lengths.shape[0]
    count_all = n_ctx * tok * n_head * (q_cols + 2 * HD)
    pieces = 2 * tok // PIECE
    vmem = pl.BlockSpec(memory_space=pltpu.VMEM)
    dq, dk, dv, rms = pl.pallas_call(
        partial(kernel, (n_ctx, n_head, n_lo, reach, docs), HD ** (-0.5), float(count_all)),
        out_shape=(
            jax.ShapeDtypeStruct((tok, q_cols), BF16),
            jax.ShapeDtypeStruct((tok, HD), BF16),
            jax.ShapeDtypeStruct((tok, HD), BF16),
            jax.ShapeDtypeStruct((8, HD), F32),
        ),
        in_specs=[pl.BlockSpec(memory_space=pltpu.SMEM)] + [vmem] * 4,
        out_specs=(vmem,) * 4,
        scratch_shapes=[
            pltpu.VMEM((reach + 1, 2 * tok, HD), BF16),
            pltpu.VMEM((reach + 1, HD, tok), BF16),
            pltpu.VMEM((HD, wide), BF16),
            pltpu.VMEM((HD, wide), BF16),
            pltpu.VMEM((wide, HD), BF16),
            pltpu.VMEM((wide, HD), BF16),
            pltpu.VMEM((reach + 1, tok, wide), F32),
            pltpu.VMEM((reach + 1, tok, wide), F32),
            pltpu.VMEM((tok, wide), BF16),
            pltpu.VMEM((tok, wide), BF16),
            pltpu.VMEM((HD, wide), F32),
            pltpu.VMEM((reach + 1, 1, wide), F32),
            pltpu.VMEM((1, wide), F32),
            pltpu.VMEM((1, wide), F32),
            pltpu.VMEM((reach + 1, 2 * tok, HD), BF16),
            pltpu.VMEM((reach + 1, 2 * tok, HD), BF16),
            pltpu.VMEM((n_head, 8, HD), F32),
            pltpu.VMEM((n_lo, 8, HD), F32),
            pltpu.VMEM((n_ctx // n_lo, 8, HD), F32),
            pltpu.SemaphoreType.DMA((reach + 1, pieces)),
            pltpu.SemaphoreType.DMA((reach + 1, pieces)),
            pltpu.SemaphoreType.DMA((reach + 1, pieces)),
            pltpu.SemaphoreType.DMA((reach + 1, pieces)),
            pltpu.SemaphoreType.DMA((3,)),
            pltpu.SemaphoreType.DMA((3,)),
        ],
        compiler_params=pltpu.CompilerParams(
            collective_id=0, has_side_effects=True, vmem_limit_bytes=40 * 1024 * 1024
        ),
        cost_estimate=pl.CostEstimate(
            flops=10 * wide * (reach + 1) * tok * HD,
            bytes_accessed=2 * 3 * tok * q_cols,
            transcendentals=wide * (reach + 1) * tok,
        ),
    )(doc_lengths, queries, keys, values, out_grad)
    return dq, dk, dv, rms[0, 0]


def solution(mesh):
    sizes = (mesh.shape["ctx"], mesh.shape["head"])
    return jax.shard_map(
        partial(local, sizes),
        mesh=mesh,
        in_specs=(P("ctx", "head"), P("ctx", "head"), P("ctx", "head"), P("ctx", "head"), P()),
        out_specs=(P("ctx", "head"), P("ctx", "head"), P("ctx", "head"), P()),
        check_vma=False,
    )
```

```python
from functools import partial

import jax
import jax.numpy as jnp
from jax import lax
from jax.experimental import pallas as pl
from jax.experimental.pallas import tpu as pltpu
from jax.sharding import PartitionSpec as P

HD = 128
LOG2E = 1.4426950408889634
MASKED = -1e30
MESH = pl.DeviceIdType.MESH
F32 = jnp.float32
BF16 = jnp.bfloat16
PIECE = 64
HOP = 5


def nn(a, b):
    return lax.dot_general(a, b, (((1,), (0,)), ((), ())), preferred_element_type=F32)


def kernel(
    sizes, scale, count_all,
    doc_ref, q_hbm, k_hbm, v_hbm, do_hbm,
    dq_ref, dk_ref, dv_ref, rms_ref,
    kv, kt, q_ref, do_ref, qt, dot_, qs, dos, p_buf, dp_buf, ds_buf, pb_buf, dqt,
    m_all, m_row, l_row, r_row, g_out, g_in,
    sum_head, sum_x, sum_z,
    load_sem, kv_send, kv_recv, g_send, g_recv, s_send, s_recv, known_sem,
):
    n_x, n_z, n_head, docs = sizes
    n_ctx = n_x * n_z
    tok = q_ref.shape[0]
    heads = q_ref.shape[1] // HD
    wide = heads * tok
    pieces = 2 * tok // PIECE
    me = lax.axis_index("ctx")
    mh = lax.axis_index("head")
    my_x = lax.div(me, n_z)
    my_z = lax.rem(me, n_z)

    def ring(step):
        return {"ctx": lax.rem(me + (step + n_ctx), n_ctx)}

    def head_partner(i):
        return {"head": lax.rem(mh + i, n_head)}

    def x_partner(i):
        return {"ctx": lax.rem(my_x + i, n_x) * n_z + my_z}

    def z_partner(i):
        return {"ctx": my_x * n_z + lax.rem(my_z + (i + n_z), n_z)}

    def tell(sem, partner):
        pl.semaphore_signal(sem, inc=1, device_id=partner, device_id_type=MESH)

    def load(i, source, target):
        return pltpu.make_async_copy(source, target, load_sem.at[i])

    loads = (
        load(0, k_hbm, kv.at[0, pl.ds(0, tok)]),
        load(1, v_hbm, kv.at[0, pl.ds(tok, tok)]),
        load(2, q_hbm, q_ref),
        load(3, do_hbm, do_ref),
    )
    for copy in loads:
        copy.start()

    barrier = pltpu.get_barrier_semaphore()
    near = [ring(1), ring(HOP), ring(-1), ring(-HOP)]
    near += [z_partner(1), z_partner(-1), z_partner(2), z_partner(-2)]
    near += [x_partner(i) for i in range(1, n_x)] + [head_partner(i) for i in range(1, n_head)]
    for partner in near:
        tell(barrier, partner)
    loads[0].wait()
    loads[1].wait()
    pl.semaphore_wait(barrier, len(near))

    def kv_copy(source, to, step, i):
        rows = pl.ds(i * PIECE, PIECE)
        return pltpu.make_async_remote_copy(
            src_ref=kv.at[source, rows],
            dst_ref=kv.at[to, rows],
            send_sem=kv_send.at[to, i],
            recv_sem=kv_recv.at[to, i],
            device_id=ring(step),
            device_id_type=MESH,
        )

    def g_copy(d, step, i):
        rows = pl.ds(i * PIECE, PIECE)
        return pltpu.make_async_remote_copy(
            src_ref=g_out.at[d, rows],
            dst_ref=g_in.at[d, rows],
            send_sem=g_send.at[d, i],
            recv_sem=g_recv.at[d, i],
            device_id=ring(step),
            device_id_type=MESH,
        )

    for i in range(pieces):
        kv_copy(0, HOP, HOP, i).start()
    for i in range(pieces):
        kv_copy(0, 1, 1, i).start()

    spans = []
    while (2 << len(spans)) < n_z // 2:
        spans.append(2 << len(spans))

    def tell_known(r):
        if r < len(spans):
            tell(known_sem.at[r], z_partner(spans[r]))
            tell(known_sem.at[r], z_partner(-spans[r]))

    def hear_known(r):
        if r < len(spans):
            pl.semaphore_wait(known_sem.at[r], 2)

    tell_known(0)

    pos = me * tok + lax.broadcasted_iota(jnp.int32, (8, tok), 1)
    first = jnp.zeros((8, tok), jnp.int32)
    begin = jnp.int32(0)
    for i in range(docs):
        first = jnp.where(begin <= pos, begin, first)
        begin = begin + doc_ref[i]
    first = first[0:1]
    pos = pos[0:1]

    loads[2].wait()
    loads[3].wait()
    for h in range(heads):
        cols = slice(h * HD, (h + 1) * HD)
        rows = slice(h * tok, (h + 1) * tok)
        qs[rows, :] = q_ref[:, cols]
        dos[rows, :] = do_ref[:, cols]
        qt[:, rows] = q_ref[:, cols].T
        dot_[:, rows] = do_ref[:, cols].T

    chunk = 256
    chunks = [slice(j, j + chunk) for j in range(0, wide, chunk)]

    def scores_of(d, opening):
        key = (me - d) * tok + lax.broadcasted_iota(jnp.int32, (tok, tok), 0)
        fine = (key >= first) & (key <= pos)
        bias = jnp.where(fine, 0.0, MASKED)
        bias = jnp.concatenate([bias] * (chunk // tok), axis=1)
        k_d = kv[d, 0:tok, :]
        v_d = kv[d, tok : 2 * tok, :]
        kt[d] = k_d.T
        for cols in chunks:
            s = nn(k_d, qt[:, cols]) * (scale * LOG2E) + bias
            top = jnp.max(s, axis=0, keepdims=True)
            if opening:
                m_new = top
            else:
                m_old = m_row[:, cols]
                m_new = jnp.maximum(m_old, top)
            p = jnp.exp2(s - m_new)
            dp = nn(v_d, dot_[:, cols])
            p_buf[d, :, cols] = p
            dp_buf[d, :, cols] = dp
            l_add = jnp.sum(p, axis=0, keepdims=True)
            r_add = jnp.sum(p * dp, axis=0, keepdims=True)
            if not opening:
                shrink = jnp.exp2(m_old - m_new)
                l_add = l_add + shrink * l_row[:, cols]
                r_add = r_add + shrink * r_row[:, cols]
            m_all[d, :, cols] = m_new
            m_row[:, cols] = m_new
            l_row[:, cols] = l_add
            r_row[:, cols] = r_add

    scores_of(0, True)

    def gather_step(j, carry):
        for d in (j, j + HOP - 1):
            for i in range(pieces):
                kv_copy(0, d, 1, i).wait_recv()

                @pl.when(j < HOP - 1)
                def _(d=d, i=i):
                    kv_copy(d, d + 1, 1, i).start()

            scores_of(d, False)
        return carry

    lax.fori_loop(1, HOP, gather_step, 0)
    hear_known(0)

    inverse = 1.0 / l_row[...]
    l_row[...] = inverse
    r_row[...] = r_row[...] * inverse

    def grads_of(d, at):
        for cols in chunks:
            factor = jnp.exp2(m_all[d, :, cols] - m_row[:, cols]) * l_row[:, cols]
            w = p_buf[d, :, cols] * factor
            pb_buf[at, :, cols] = w.astype(BF16)
            ds_buf[at, :, cols] = (w * (dp_buf[d, :, cols] - r_row[:, cols])).astype(BF16)
        dk = nn(ds_buf[at], qs[...]) * scale
        dv = nn(pb_buf[at], dos[...])
        return dk, dv

    def queries_of(d, at, opening):
        for cols in chunks:
            part = nn(kt[d], ds_buf[at, :, cols])
            if opening:
                dqt[:, cols] = part
            else:
                dqt[:, cols] = dqt[:, cols] + part

    def piece_of(dk, dv, i):
        whole, begin = (dk, i * PIECE) if i * PIECE < tok else (dv, i * PIECE - tok)
        return whole[begin : begin + PIECE]

    def return_pair(j, opening, last):
        far, close = 2 * (HOP - 1) - j, HOP - 1 - j
        for at, d in enumerate((far, close)):
            dk, dv = grads_of(d, at)
            step = -HOP if last and at == 0 else -1
            for i in range(pieces):
                rows = slice(i * PIECE, (i + 1) * PIECE)
                part = piece_of(dk, dv, i)
                if not opening:
                    g_copy(d + 1, -1, i).wait_recv()
                    part = part + g_in[d + 1, rows, :].astype(F32)
                g_out[d, rows, :] = part.astype(BF16)
                g_copy(d, step, i).start()
        queries_of(far, 0, opening)
        queries_of(close, 1, False)

    return_pair(0, True, False)
    tell_known(1)

    def return_step(j, carry):
        return_pair(j, False, False)
        return carry

    lax.fori_loop(1, HOP - 2, return_step, 0)
    return_pair(HOP - 2, False, True)
    hear_known(1)
    tell_known(2)
    dk, dv = grads_of(0, 0)
    queries_of(0, 0, False)
    squares = jnp.zeros((8, HD), F32)
    for h in range(heads):
        part = dqt[:, h * tok : (h + 1) * tok] * scale
        squares = squares + jnp.sum((part * part).reshape(HD // 8, 8, tok), axis=0)
        dq_ref[:, h * HD : (h + 1) * HD] = part.T.astype(BF16)
    hear_known(2)
    for i in range(pieces):
        rows = slice(i * PIECE, (i + 1) * PIECE)
        g_copy(1, -1, i).wait_recv()
        g_copy(HOP, -HOP, i).wait_recv()
        part = piece_of(dk, dv, i) + g_in[1, rows, :].astype(F32) + g_in[HOP, rows, :].astype(F32)
        squares = squares + jnp.sum((part * part).reshape(PIECE // 8, 8, HD), axis=0)
        out, begin = (dk_ref, i * PIECE) if i * PIECE < tok else (dv_ref, i * PIECE - tok)
        out[begin : begin + PIECE, :] = part.astype(BF16)

    levels = (
        (head_partner, range(1, n_head), mh, sum_head),
        (x_partner, range(1, n_x), my_x, sum_x),
        (z_partner, sorted(range(1, n_z), key=lambda i: -min(i, n_z - i)), my_z, sum_z),
    )
    for level, (partner, offsets, mine, slots) in enumerate(levels):
        n = slots.shape[0]
        slots[mine] = squares
        for i in offsets:
            pltpu.make_async_remote_copy(
                src_ref=slots.at[mine],
                dst_ref=slots.at[mine],
                send_sem=s_send.at[level],
                recv_sem=s_recv.at[level],
                device_id=partner(i),
                device_id_type=MESH,
            ).start()
        if n > 1:
            others = slots.at[pl.ds(0, n - 1)]
            pltpu.make_async_copy(others, others, s_recv.at[level]).wait()
        squares = slots[0]
        for i in range(1, n):
            squares = squares + slots[i]
    rms_ref[...] = jnp.broadcast_to(jnp.sqrt(jnp.sum(squares) / count_all), rms_ref.shape)

    for level, (_, _, _, slots) in enumerate(levels):
        n = slots.shape[0]
        if n > 1:
            others = slots.at[pl.ds(0, n - 1)]
            pltpu.make_async_copy(others, others, s_send.at[level]).wait()
    for d in range(1, 2 * HOP - 1):
        for i in range(pieces):
            kv_copy(0, d, 1, i).wait_send()
            g_copy(d, -1, i).wait_send()


def local(mesh_sizes, queries, keys, values, out_grad, doc_lengths):
    n_ctx, n_head = mesh_sizes
    tok, q_cols = queries.shape
    wide = q_cols // HD * tok
    n_x = 4 if n_ctx == 128 else 2
    n_z = n_ctx // n_x
    blocks = 2 * (HOP - 1) + 1
    docs = doc_lengths.shape[0]
    count_all = n_ctx * tok * n_head * (q_cols + 2 * HD)
    pieces = 2 * tok // PIECE
    vmem = pl.BlockSpec(memory_space=pltpu.VMEM)
    dq, dk, dv, rms = pl.pallas_call(
        partial(kernel, (n_x, n_z, n_head, docs), HD ** (-0.5), float(count_all)),
        out_shape=(
            jax.ShapeDtypeStruct((tok, q_cols), BF16),
            jax.ShapeDtypeStruct((tok, HD), BF16),
            jax.ShapeDtypeStruct((tok, HD), BF16),
            jax.ShapeDtypeStruct((8, HD), F32),
        ),
        in_specs=[pl.BlockSpec(memory_space=pltpu.SMEM)] + [pl.BlockSpec(memory_space=pl.ANY)] * 4,
        out_specs=(vmem,) * 4,
        scratch_shapes=[
            pltpu.VMEM((blocks, 2 * tok, HD), BF16),
            pltpu.VMEM((blocks, HD, tok), BF16),
            pltpu.VMEM((tok, q_cols), BF16),
            pltpu.VMEM((tok, q_cols), BF16),
            pltpu.VMEM((HD, wide), BF16),
            pltpu.VMEM((HD, wide), BF16),
            pltpu.VMEM((wide, HD), BF16),
            pltpu.VMEM((wide, HD), BF16),
            pltpu.VMEM((blocks, tok, wide), F32),
            pltpu.VMEM((blocks, tok, wide), F32),
            pltpu.VMEM((2, tok, wide), BF16),
            pltpu.VMEM((2, tok, wide), BF16),
            pltpu.VMEM((HD, wide), F32),
            pltpu.VMEM((blocks, 1, wide), F32),
            pltpu.VMEM((1, wide), F32),
            pltpu.VMEM((1, wide), F32),
            pltpu.VMEM((1, wide), F32),
            pltpu.VMEM((blocks, 2 * tok, HD), BF16),
            pltpu.VMEM((blocks, 2 * tok, HD), BF16),
            pltpu.VMEM((n_head, 8, HD), F32),
            pltpu.VMEM((n_x, 8, HD), F32),
            pltpu.VMEM((n_z, 8, HD), F32),
            pltpu.SemaphoreType.DMA((4,)),
            pltpu.SemaphoreType.DMA((blocks, pieces)),
            pltpu.SemaphoreType.DMA((blocks, pieces)),
            pltpu.SemaphoreType.DMA((blocks, pieces)),
            pltpu.SemaphoreType.DMA((blocks, pieces)),
            pltpu.SemaphoreType.DMA((3,)),
            pltpu.SemaphoreType.DMA((3,)),
            pltpu.SemaphoreType.REGULAR((3,)),
        ],
        compiler_params=pltpu.CompilerParams(
            collective_id=0, has_side_effects=True, vmem_limit_bytes=56 * 1024 * 1024
        ),
        cost_estimate=pl.CostEstimate(
            flops=10 * wide * blocks * tok * HD,
            bytes_accessed=2 * 3 * tok * q_cols,
            transcendentals=wide * blocks * tok,
        ),
    )(doc_lengths, queries, keys, values, out_grad)
    return dq, dk, dv, rms[0, 0]


def solution(mesh):
    sizes = (mesh.shape["ctx"], mesh.shape["head"])
    return jax.shard_map(
        partial(local, sizes),
        mesh=mesh,
        in_specs=(P("ctx", "head"), P("ctx", "head"), P("ctx", "head"), P("ctx", "head"), P()),
        out_specs=(P("ctx", "head"), P("ctx", "head"), P("ctx", "head"), P()),
        check_vma=False,
    )
```

```python
from functools import partial

import jax
import jax.numpy as jnp
from jax import lax
from jax.experimental import pallas as pl
from jax.experimental.pallas import tpu as pltpu
from jax.sharding import PartitionSpec as P

HD = 128
LOG2E = 1.4426950408889634
MASKED = -1e30
MESH = pl.DeviceIdType.MESH
F32 = jnp.float32
BF16 = jnp.bfloat16
PIECE = 64
HOP = 5


def nn(a, b):
    return lax.dot_general(a, b, (((1,), (0,)), ((), ())), preferred_element_type=F32)


def kernel(
    sizes, scale, count_all,
    doc_ref, q_hbm, k_hbm, v_hbm, do_hbm,
    dq_ref, dk_ref, dv_ref, rms_ref,
    kv, kt, q_ref, do_ref, qt, dot_, qs, dos, p_buf, dp_buf, ds_buf, pb_buf, dqt,
    m_all, m_row, l_row, r_row, g_out, g_in,
    sum_plane, sum_z,
    load_sem, kv_send, kv_recv, g_send, g_recv, s_send, s_recv, known_sem,
):
    n_x, n_z, n_head, docs = sizes
    n_ctx = n_x * n_z
    tok = q_ref.shape[0]
    heads = q_ref.shape[1] // HD
    wide = heads * tok
    pieces = 2 * tok // PIECE
    me = lax.axis_index("ctx")
    mh = lax.axis_index("head")
    my_x = lax.div(me, n_z)
    my_z = lax.rem(me, n_z)

    def ring(step):
        return {"ctx": lax.rem(me + (step + n_ctx), n_ctx)}

    def head_partner(i):
        return {"head": lax.rem(mh + i, n_head)}

    def x_partner(i):
        return {"ctx": lax.rem(my_x + i, n_x) * n_z + my_z}

    def plane_partner(i):
        return x_partner(i // n_head) | head_partner(i % n_head)

    def z_partner(i):
        return {"ctx": my_x * n_z + lax.rem(my_z + (i + n_z), n_z)}

    def tell(sem, partner):
        pl.semaphore_signal(sem, inc=1, device_id=partner, device_id_type=MESH)

    def load(i, source, target):
        return pltpu.make_async_copy(source, target, load_sem.at[i])

    loads = (
        load(0, k_hbm, kv.at[0, pl.ds(0, tok)]),
        load(1, v_hbm, kv.at[0, pl.ds(tok, tok)]),
        load(2, q_hbm, q_ref),
        load(3, do_hbm, do_ref),
    )
    for copy in loads:
        copy.start()

    barrier = pltpu.get_barrier_semaphore()
    near = [ring(-HOP), ring(HOP), ring(-1), ring(1)]
    near += [x_partner(i) for i in range(1, n_x)] + [head_partner(i) for i in range(1, n_head)]
    near += [z_partner(2), z_partner(-2), z_partner(1), z_partner(-1)]
    for partner in near:
        tell(barrier, partner)
    loads[0].wait()
    loads[1].wait()
    pl.semaphore_wait(barrier, len(near))

    def kv_copy(source, to, step, i):
        rows = pl.ds(i * PIECE, PIECE)
        return pltpu.make_async_remote_copy(
            src_ref=kv.at[source, rows],
            dst_ref=kv.at[to, rows],
            send_sem=kv_send.at[to, i],
            recv_sem=kv_recv.at[to, i],
            device_id=ring(step),
            device_id_type=MESH,
        )

    def g_copy(d, step, i):
        rows = pl.ds(i * PIECE, PIECE)
        return pltpu.make_async_remote_copy(
            src_ref=g_out.at[d, rows],
            dst_ref=g_in.at[d, rows],
            send_sem=g_send.at[d, i],
            recv_sem=g_recv.at[d, i],
            device_id=ring(step),
            device_id_type=MESH,
        )

    for i in range(pieces):
        kv_copy(0, HOP, HOP, i).start()
    for i in range(pieces):
        kv_copy(0, 1, 1, i).start()

    spans = []
    while (2 << len(spans)) < n_z // 2:
        spans.append(2 << len(spans))

    def tell_known(r):
        if r < len(spans):
            tell(known_sem.at[r], z_partner(spans[r]))
            tell(known_sem.at[r], z_partner(-spans[r]))

    def hear_known(r):
        if r < len(spans):
            pl.semaphore_wait(known_sem.at[r], 2)

    tell_known(0)
    for i in range(1, n_x):
        tell(known_sem.at[3], x_partner(i))

    pos = me * tok + lax.broadcasted_iota(jnp.int32, (8, tok), 1)
    first = jnp.zeros((8, tok), jnp.int32)
    begin = jnp.int32(0)
    for i in range(docs):
        first = jnp.where(begin <= pos, begin, first)
        begin = begin + doc_ref[i]
    first = first[0:1]
    pos = pos[0:1]

    loads[2].wait()
    loads[3].wait()
    for h in range(heads):
        cols = slice(h * HD, (h + 1) * HD)
        rows = slice(h * tok, (h + 1) * tok)
        qs[rows, :] = q_ref[:, cols]
        dos[rows, :] = do_ref[:, cols]
        qt[:, rows] = q_ref[:, cols].T
        dot_[:, rows] = do_ref[:, cols].T

    chunk = 256
    chunks = [slice(j, j + chunk) for j in range(0, wide, chunk)]

    def scores_of(d, opening):
        key = (me - d) * tok + lax.broadcasted_iota(jnp.int32, (tok, tok), 0)
        fine = (key >= first) & (key <= pos)
        bias = jnp.where(fine, 0.0, MASKED)
        bias = jnp.concatenate([bias] * (chunk // tok), axis=1)
        k_d = kv[d, 0:tok, :]
        v_d = kv[d, tok : 2 * tok, :]
        kt[d] = k_d.T
        for cols in chunks:
            s = nn(k_d, qt[:, cols]) * (scale * LOG2E) + bias
            top = jnp.max(s, axis=0, keepdims=True)
            if opening:
                m_new = top
            else:
                m_old = m_row[:, cols]
                m_new = jnp.maximum(m_old, top)
            p = jnp.exp2(s - m_new)
            dp = nn(v_d, dot_[:, cols])
            p_buf[d, :, cols] = p
            dp_buf[d, :, cols] = dp
            l_add = jnp.sum(p, axis=0, keepdims=True)
            r_add = jnp.sum(p * dp, axis=0, keepdims=True)
            if not opening:
                shrink = jnp.exp2(m_old - m_new)
                l_add = l_add + shrink * l_row[:, cols]
                r_add = r_add + shrink * r_row[:, cols]
            m_all[d, :, cols] = m_new
            m_row[:, cols] = m_new
            l_row[:, cols] = l_add
            r_row[:, cols] = r_add

    scores_of(0, True)

    def gather_step(j, carry):
        for d in (j, j + HOP - 1):
            for i in range(pieces):
                kv_copy(0, d, 1, i).wait_recv()

                @pl.when(j < HOP - 1)
                def _(d=d, i=i):
                    kv_copy(d, d + 1, 1, i).start()

            scores_of(d, False)
        return carry

    lax.fori_loop(1, HOP, gather_step, 0)
    hear_known(0)

    inverse = 1.0 / l_row[...]
    l_row[...] = inverse
    r_row[...] = r_row[...] * inverse

    def grads_of(d, at):
        for cols in chunks:
            factor = jnp.exp2(m_all[d, :, cols] - m_row[:, cols]) * l_row[:, cols]
            w = p_buf[d, :, cols] * factor
            pb_buf[at, :, cols] = w.astype(BF16)
            ds_buf[at, :, cols] = (w * (dp_buf[d, :, cols] - r_row[:, cols])).astype(BF16)
        dk = nn(ds_buf[at], qs[...]) * scale
        dv = nn(pb_buf[at], dos[...])
        return dk, dv

    def queries_of(d, at, opening):
        for cols in chunks:
            part = nn(kt[d], ds_buf[at, :, cols])
            if opening:
                dqt[:, cols] = part
            else:
                dqt[:, cols] = dqt[:, cols] + part

    def piece_of(dk, dv, i):
        whole, begin = (dk, i * PIECE) if i * PIECE < tok else (dv, i * PIECE - tok)
        return whole[begin : begin + PIECE]

    def return_pair(j, opening, last):
        far, close = 2 * (HOP - 1) - j, HOP - 1 - j
        for at, d in enumerate((far, close)):
            dk, dv = grads_of(d, at)
            step = -HOP if last and at == 0 else -1
            for i in range(pieces):
                rows = slice(i * PIECE, (i + 1) * PIECE)
                part = piece_of(dk, dv, i)
                if not opening:
                    g_copy(d + 1, -1, i).wait_recv()
                    part = part + g_in[d + 1, rows, :].astype(F32)
                g_out[d, rows, :] = part.astype(BF16)
                g_copy(d, step, i).start()
        queries_of(far, 0, opening)
        queries_of(close, 1, False)

    return_pair(0, True, False)
    tell_known(1)

    def return_step(j, carry):
        return_pair(j, False, False)
        return carry

    lax.fori_loop(1, HOP - 2, return_step, 0)
    return_pair(HOP - 2, False, True)
    hear_known(1)
    tell_known(2)
    dk, dv = grads_of(0, 0)
    queries_of(0, 0, False)
    squares = jnp.zeros((8, HD), F32)
    for h in range(heads):
        part = dqt[:, h * tok : (h + 1) * tok] * scale
        squares = squares + jnp.sum((part * part).reshape(HD // 8, 8, tok), axis=0)
        dq_ref[:, h * HD : (h + 1) * HD] = part.T.astype(BF16)
    hear_known(2)
    if n_x > 1:
        pl.semaphore_wait(known_sem.at[3], n_x - 1)
    for i in range(pieces):
        rows = slice(i * PIECE, (i + 1) * PIECE)
        g_copy(1, -1, i).wait_recv()
        g_copy(HOP, -HOP, i).wait_recv()
        part = piece_of(dk, dv, i) + g_in[1, rows, :].astype(F32) + g_in[HOP, rows, :].astype(F32)
        squares = squares + jnp.sum((part * part).reshape(PIECE // 8, 8, HD), axis=0)
        out, begin = (dk_ref, i * PIECE) if i * PIECE < tok else (dv_ref, i * PIECE - tok)
        out[begin : begin + PIECE, :] = part.astype(BF16)

    def away(i, n):
        return min(i % n, n - i % n)

    def plane_away(i):
        return -away(i // n_head, n_x) - away(i % n_head // 2, max(n_head // 2, 1))

    levels = (
        (plane_partner, sorted(range(1, n_x * n_head), key=plane_away), my_x * n_head + mh, sum_plane),
        (z_partner, sorted(range(1, n_z), key=lambda i: -away(i, n_z)), my_z, sum_z),
    )
    for level, (partner, offsets, mine, slots) in enumerate(levels):
        n = slots.shape[0]
        slots[mine] = squares
        for i in offsets:
            pltpu.make_async_remote_copy(
                src_ref=slots.at[mine],
                dst_ref=slots.at[mine],
                send_sem=s_send.at[level],
                recv_sem=s_recv.at[level],
                device_id=partner(i),
                device_id_type=MESH,
            ).start()
        if level == 1:
            for d in range(1, 2 * HOP - 1):
                for i in range(pieces):
                    kv_copy(0, d, 1, i).wait_send()
                    g_copy(d, -1, i).wait_send()
        others = slots.at[pl.ds(0, n - 1)]
        pltpu.make_async_copy(others, others, s_recv.at[level]).wait()
        parts = [slots[i] for i in range(n)]
        while len(parts) > 1:
            parts = [sum(parts[i : i + 2][1:], parts[i]) for i in range(0, len(parts), 2)]
        squares = parts[0]
    rms_ref[...] = jnp.broadcast_to(jnp.sqrt(jnp.sum(squares) / count_all), rms_ref.shape)

    for level, (_, _, _, slots) in enumerate(levels):
        others = slots.at[pl.ds(0, slots.shape[0] - 1)]
        pltpu.make_async_copy(others, others, s_send.at[level]).wait()


def local(mesh_sizes, queries, keys, values, out_grad, doc_lengths):
    n_ctx, n_head = mesh_sizes
    tok, q_cols = queries.shape
    wide = q_cols // HD * tok
    n_x = 4 if n_ctx == 128 else 2
    n_z = n_ctx // n_x
    blocks = 2 * (HOP - 1) + 1
    docs = doc_lengths.shape[0]
    count_all = n_ctx * tok * n_head * (q_cols + 2 * HD)
    pieces = 2 * tok // PIECE
    vmem = pl.BlockSpec(memory_space=pltpu.VMEM)
    dq, dk, dv, rms = pl.pallas_call(
        partial(kernel, (n_x, n_z, n_head, docs), HD ** (-0.5), float(count_all)),
        out_shape=(
            pltpu.VMEM((tok, q_cols), BF16),
            pltpu.VMEM((tok, HD), BF16),
            pltpu.VMEM((tok, HD), BF16),
            pltpu.VMEM((8, HD), F32),
        ),
        in_specs=[pl.BlockSpec(memory_space=pltpu.SMEM)] + [pl.BlockSpec(memory_space=pl.ANY)] * 4,
        out_specs=(vmem,) * 4,
        scratch_shapes=[
            pltpu.VMEM((blocks, 2 * tok, HD), BF16),
            pltpu.VMEM((blocks, HD, tok), BF16),
            pltpu.VMEM((tok, q_cols), BF16),
            pltpu.VMEM((tok, q_cols), BF16),
            pltpu.VMEM((HD, wide), BF16),
            pltpu.VMEM((HD, wide), BF16),
            pltpu.VMEM((wide, HD), BF16),
            pltpu.VMEM((wide, HD), BF16),
            pltpu.VMEM((blocks, tok, wide), F32),
            pltpu.VMEM((blocks, tok, wide), F32),
            pltpu.VMEM((2, tok, wide), BF16),
            pltpu.VMEM((2, tok, wide), BF16),
            pltpu.VMEM((HD, wide), F32),
            pltpu.VMEM((blocks, 1, wide), F32),
            pltpu.VMEM((1, wide), F32),
            pltpu.VMEM((1, wide), F32),
            pltpu.VMEM((1, wide), F32),
            pltpu.VMEM((blocks, 2 * tok, HD), BF16),
            pltpu.VMEM((blocks, 2 * tok, HD), BF16),
            pltpu.VMEM((n_x * n_head, 8, HD), F32),
            pltpu.VMEM((n_z, 8, HD), F32),
            pltpu.SemaphoreType.DMA((4,)),
            pltpu.SemaphoreType.DMA((blocks, pieces)),
            pltpu.SemaphoreType.DMA((blocks, pieces)),
            pltpu.SemaphoreType.DMA((blocks, pieces)),
            pltpu.SemaphoreType.DMA((blocks, pieces)),
            pltpu.SemaphoreType.DMA((2,)),
            pltpu.SemaphoreType.DMA((2,)),
            pltpu.SemaphoreType.REGULAR((4,)),
        ],
        compiler_params=pltpu.CompilerParams(
            collective_id=0, has_side_effects=True, vmem_limit_bytes=56 * 1024 * 1024
        ),
        cost_estimate=pl.CostEstimate(
            flops=10 * wide * blocks * tok * HD,
            bytes_accessed=2 * 3 * tok * q_cols,
            transcendentals=wide * blocks * tok,
        ),
    )(doc_lengths, queries, keys, values, out_grad)
    return dq, dk, dv, rms[0, 0]


def solution(mesh):
    sizes = (mesh.shape["ctx"], mesh.shape["head"])
    return jax.shard_map(
        partial(local, sizes),
        mesh=mesh,
        in_specs=(P("ctx", "head"), P("ctx", "head"), P("ctx", "head"), P("ctx", "head"), P()),
        out_specs=(P("ctx", "head"), P("ctx", "head"), P("ctx", "head"), P()),
        check_vma=False,
    )
```

```python
from functools import partial

import jax
import jax.numpy as jnp
from jax import lax
from jax.experimental import pallas as pl
from jax.experimental.pallas import tpu as pltpu
from jax.sharding import PartitionSpec as P

HD = 128
LOG2E = 1.4426950408889634
MASKED = -1e30
MESH = pl.DeviceIdType.MESH
F32 = jnp.float32
BF16 = jnp.bfloat16
PIECE = 64
HOP = 5


def nn(a, b):
    return lax.dot_general(a, b, (((1,), (0,)), ((), ())), preferred_element_type=F32)


def kernel(
    sizes, scale, count_all,
    doc_ref, q_hbm, k_hbm, v_hbm, do_hbm,
    dq_ref, dk_ref, dv_ref, rms_ref,
    kv, kt, q_ref, do_ref, qt, dot_, qs, dos, p_buf, dp_buf, ds_buf, pb_buf, dqt,
    m_all, m_row, l_row, r_row, g_out, g_in,
    sum_plane, sum_z,
    load_sem, kv_send, kv_recv, g_send, g_recv, s_send, s_recv, known_sem,
):
    n_x, n_z, n_head, docs = sizes
    n_ctx = n_x * n_z
    tok = q_ref.shape[0]
    heads = q_ref.shape[1] // HD
    wide = heads * tok
    pieces = 2 * tok // PIECE
    me = lax.axis_index("ctx")
    mh = lax.axis_index("head")
    my_x = lax.div(me, n_z)
    my_z = lax.rem(me, n_z)

    def ring(step):
        return {"ctx": lax.rem(me + (step + n_ctx), n_ctx)}

    def head_partner(i):
        return {"head": lax.rem(mh + i, n_head)}

    def x_partner(i):
        return {"ctx": lax.rem(my_x + i, n_x) * n_z + my_z}

    def plane_partner(i):
        return x_partner(i // n_head) | head_partner(i % n_head)

    def z_partner(i):
        return {"ctx": my_x * n_z + lax.rem(my_z + (i + n_z), n_z)}

    def tell(sem, partner):
        pl.semaphore_signal(sem, inc=1, device_id=partner, device_id_type=MESH)

    def load(i, source, target):
        return pltpu.make_async_copy(source, target, load_sem.at[i])

    loads = (
        load(0, k_hbm, kv.at[0, pl.ds(0, tok)]),
        load(1, v_hbm, kv.at[0, pl.ds(tok, tok)]),
        load(2, q_hbm, q_ref),
        load(3, do_hbm, do_ref),
    )
    for copy in loads:
        copy.start()

    barrier = pltpu.get_barrier_semaphore()
    near = [ring(-HOP), ring(HOP), ring(-1), ring(1)]
    near += [x_partner(i) for i in range(1, n_x)] + [head_partner(i) for i in range(1, n_head)]
    near += [z_partner(2), z_partner(-2), z_partner(1), z_partner(-1)]
    for partner in near:
        tell(barrier, partner)
    loads[0].wait()
    loads[1].wait()
    pl.semaphore_wait(barrier, len(near))

    def kv_copy(source, to, step, i):
        rows = pl.ds(i * PIECE, PIECE)
        return pltpu.make_async_remote_copy(
            src_ref=kv.at[source, rows],
            dst_ref=kv.at[to, rows],
            send_sem=kv_send.at[to, i],
            recv_sem=kv_recv.at[to, i],
            device_id=ring(step),
            device_id_type=MESH,
        )

    def g_copy(d, step, i):
        rows = pl.ds(i * PIECE, PIECE)
        return pltpu.make_async_remote_copy(
            src_ref=g_out.at[d, rows],
            dst_ref=g_in.at[d, rows],
            send_sem=g_send.at[d, i],
            recv_sem=g_recv.at[d, i],
            device_id=ring(step),
            device_id_type=MESH,
        )

    for i in range(pieces):
        kv_copy(0, HOP, HOP, i).start()
    for i in range(pieces):
        kv_copy(0, 1, 1, i).start()

    spans = []
    while (2 << len(spans)) < n_z // 2:
        spans.append(2 << len(spans))

    def tell_known(r):
        if r < len(spans):
            tell(known_sem.at[r], z_partner(spans[r]))
            tell(known_sem.at[r], z_partner(-spans[r]))

    def hear_known(r):
        if r < len(spans):
            pl.semaphore_wait(known_sem.at[r], 2)

    tell_known(0)
    for i in range(1, n_x):
        tell(known_sem.at[3], x_partner(i))

    pos = me * tok + lax.broadcasted_iota(jnp.int32, (8, tok), 1)
    first = jnp.zeros((8, tok), jnp.int32)
    begin = jnp.int32(0)
    for i in range(docs):
        first = jnp.where(begin <= pos, begin, first)
        begin = begin + doc_ref[i]
    first = first[0:1]
    pos = pos[0:1]

    loads[2].wait()
    loads[3].wait()
    for h in range(heads):
        cols = slice(h * HD, (h + 1) * HD)
        rows = slice(h * tok, (h + 1) * tok)
        qs[rows, :] = q_ref[:, cols]
        dos[rows, :] = do_ref[:, cols]
        qt[:, rows] = q_ref[:, cols].T
        dot_[:, rows] = do_ref[:, cols].T

    chunk = 256
    chunks = [slice(j, j + chunk) for j in range(0, wide, chunk)]

    def scores_of(d, opening):
        key = (me - d) * tok + lax.broadcasted_iota(jnp.int32, (tok, tok), 0)
        fine = (key >= first) & (key <= pos)
        bias = jnp.where(fine, 0.0, MASKED)
        bias = jnp.concatenate([bias] * (chunk // tok), axis=1)
        k_d = kv[d, 0:tok, :]
        v_d = kv[d, tok : 2 * tok, :]
        kt[d] = k_d.T
        for cols in chunks:
            s = nn(k_d, qt[:, cols]) * (scale * LOG2E) + bias
            top = jnp.max(s, axis=0, keepdims=True)
            if opening:
                m_new = top
            else:
                m_old = m_row[:, cols]
                m_new = jnp.maximum(m_old, top)
            p = jnp.exp2(s - m_new)
            dp = nn(v_d, dot_[:, cols])
            p_buf[d, :, cols] = p
            dp_buf[d, :, cols] = dp
            l_add = jnp.sum(p, axis=0, keepdims=True)
            r_add = jnp.sum(p * dp, axis=0, keepdims=True)
            if not opening:
                shrink = jnp.exp2(m_old - m_new)
                l_add = l_add + shrink * l_row[:, cols]
                r_add = r_add + shrink * r_row[:, cols]
            m_all[d, :, cols] = m_new
            m_row[:, cols] = m_new
            l_row[:, cols] = l_add
            r_row[:, cols] = r_add

    scores_of(0, True)

    def gather_step(j, carry):
        for d in (j, j + HOP - 1):
            for i in range(pieces):
                kv_copy(0, d, 1, i).wait_recv()

                @pl.when(j < HOP - 1)
                def _(d=d, i=i):
                    kv_copy(d, d + 1, 1, i).start()

            scores_of(d, False)
        return carry

    lax.fori_loop(1, HOP, gather_step, 0)
    hear_known(0)

    inverse = 1.0 / l_row[...]
    l_row[...] = inverse
    r_row[...] = r_row[...] * inverse

    def grads_of(d, at):
        for cols in chunks:
            factor = jnp.exp2(m_all[d, :, cols] - m_row[:, cols]) * l_row[:, cols]
            w = p_buf[d, :, cols] * factor
            pb_buf[at, :, cols] = w.astype(BF16)
            ds_buf[at, :, cols] = (w * (dp_buf[d, :, cols] - r_row[:, cols])).astype(BF16)
        dk = nn(ds_buf[at], qs[...]) * scale
        dv = nn(pb_buf[at], dos[...])
        return dk, dv

    def queries_of(d, at, opening):
        for cols in chunks:
            part = nn(kt[d], ds_buf[at, :, cols])
            if opening:
                dqt[:, cols] = part
            else:
                dqt[:, cols] = dqt[:, cols] + part

    def piece_of(dk, dv, i):
        whole, begin = (dk, i * PIECE) if i * PIECE < tok else (dv, i * PIECE - tok)
        return whole[begin : begin + PIECE]

    def return_pair(j, opening, last):
        far, close = 2 * (HOP - 1) - j, HOP - 1 - j
        for at, d in enumerate((far, close)):
            dk, dv = grads_of(d, at)
            step = -HOP if last and at == 0 else -1
            for i in range(pieces):
                rows = slice(i * PIECE, (i + 1) * PIECE)
                part = piece_of(dk, dv, i)
                if not opening:
                    g_copy(d + 1, -1, i).wait_recv()
                    part = part + g_in[d + 1, rows, :].astype(F32)
                g_out[d, rows, :] = part.astype(BF16)
                g_copy(d, step, i).start()
        queries_of(far, 0, opening)
        queries_of(close, 1, False)

    return_pair(0, True, False)
    tell_known(1)

    def return_step(j, carry):
        return_pair(j, False, False)
        return carry

    lax.fori_loop(1, HOP - 2, return_step, 0)
    return_pair(HOP - 2, False, True)
    hear_known(1)
    tell_known(2)
    dk, dv = grads_of(0, 0)
    queries_of(0, 0, False)
    squares = jnp.zeros((8, HD), F32)
    for h in range(heads):
        part = dqt[:, h * tok : (h + 1) * tok] * scale
        squares = squares + jnp.sum((part * part).reshape(HD // 8, 8, tok), axis=0)
        dq_ref[:, h * HD : (h + 1) * HD] = part.T.astype(BF16)
    hear_known(2)
    if n_x > 1:
        pl.semaphore_wait(known_sem.at[3], n_x - 1)
    for i in range(pieces):
        rows = slice(i * PIECE, (i + 1) * PIECE)
        g_copy(1, -1, i).wait_recv()
        g_copy(HOP, -HOP, i).wait_recv()
        part = piece_of(dk, dv, i) + g_in[1, rows, :].astype(F32) + g_in[HOP, rows, :].astype(F32)
        squares = squares + jnp.sum((part * part).reshape(PIECE // 8, 8, HD), axis=0)
        out, begin = (dk_ref, i * PIECE) if i * PIECE < tok else (dv_ref, i * PIECE - tok)
        out[begin : begin + PIECE, :] = part.astype(BF16)

    def away(i, n):
        return min(i % n, n - i % n)

    def plane_away(i):
        return -away(i // n_head, n_x) - away(i % n_head // 2, max(n_head // 2, 1))

    levels = (
        (plane_partner, sorted(range(1, n_x * n_head), key=plane_away), my_x * n_head + mh, sum_plane),
        (z_partner, sorted(range(1, n_z), key=lambda i: -away(i, n_z)), my_z, sum_z),
    )
    for level, (partner, offsets, mine, slots) in enumerate(levels):
        n = slots.shape[0]
        slots[mine] = jnp.sum(squares, axis=0, keepdims=True)
        for i in offsets:
            pltpu.make_async_remote_copy(
                src_ref=slots.at[mine],
                dst_ref=slots.at[mine],
                send_sem=s_send.at[level],
                recv_sem=s_recv.at[level],
                device_id=partner(i),
                device_id_type=MESH,
            ).start()
        if level == 1:
            for d in range(1, 2 * HOP - 1):
                for i in range(pieces):
                    kv_copy(0, d, 1, i).wait_send()
                    g_copy(d, -1, i).wait_send()
        others = slots.at[pl.ds(0, n - 1)]
        pltpu.make_async_copy(others, others, s_recv.at[level]).wait()
        parts = [slots[i] for i in range(n)]
        while len(parts) > 1:
            parts = [sum(parts[i : i + 2][1:], parts[i]) for i in range(0, len(parts), 2)]
        squares = parts[0]
    rms_ref[...] = jnp.broadcast_to(jnp.sqrt(jnp.sum(squares) / count_all), rms_ref.shape)

    for level, (_, _, _, slots) in enumerate(levels):
        others = slots.at[pl.ds(0, slots.shape[0] - 1)]
        pltpu.make_async_copy(others, others, s_send.at[level]).wait()


def local(mesh_sizes, queries, keys, values, out_grad, doc_lengths):
    n_ctx, n_head = mesh_sizes
    tok, q_cols = queries.shape
    wide = q_cols // HD * tok
    n_x = 4 if n_ctx == 128 else 2
    n_z = n_ctx // n_x
    blocks = 2 * (HOP - 1) + 1
    docs = doc_lengths.shape[0]
    count_all = n_ctx * tok * n_head * (q_cols + 2 * HD)
    pieces = 2 * tok // PIECE
    vmem = pl.BlockSpec(memory_space=pltpu.VMEM)
    dq, dk, dv, rms = pl.pallas_call(
        partial(kernel, (n_x, n_z, n_head, docs), HD ** (-0.5), float(count_all)),
        out_shape=(
            pltpu.VMEM((tok, q_cols), BF16),
            pltpu.VMEM((tok, HD), BF16),
            pltpu.VMEM((tok, HD), BF16),
            pltpu.VMEM((8, HD), F32),
        ),
        in_specs=[pl.BlockSpec(memory_space=pltpu.SMEM)] + [pl.BlockSpec(memory_space=pl.ANY)] * 4,
        out_specs=(vmem,) * 4,
        scratch_shapes=[
            pltpu.VMEM((blocks, 2 * tok, HD), BF16),
            pltpu.VMEM((blocks, HD, tok), BF16),
            pltpu.VMEM((tok, q_cols), BF16),
            pltpu.VMEM((tok, q_cols), BF16),
            pltpu.VMEM((HD, wide), BF16),
            pltpu.VMEM((HD, wide), BF16),
            pltpu.VMEM((wide, HD), BF16),
            pltpu.VMEM((wide, HD), BF16),
            pltpu.VMEM((blocks, tok, wide), F32),
            pltpu.VMEM((blocks, tok, wide), F32),
            pltpu.VMEM((2, tok, wide), BF16),
            pltpu.VMEM((2, tok, wide), BF16),
            pltpu.VMEM((HD, wide), F32),
            pltpu.VMEM((blocks, 1, wide), F32),
            pltpu.VMEM((1, wide), F32),
            pltpu.VMEM((1, wide), F32),
            pltpu.VMEM((1, wide), F32),
            pltpu.VMEM((blocks, 2 * tok, HD), BF16),
            pltpu.VMEM((blocks, 2 * tok, HD), BF16),
            pltpu.VMEM((n_x * n_head, 1, HD), F32),
            pltpu.VMEM((n_z, 1, HD), F32),
            pltpu.SemaphoreType.DMA((4,)),
            pltpu.SemaphoreType.DMA((blocks, pieces)),
            pltpu.SemaphoreType.DMA((blocks, pieces)),
            pltpu.SemaphoreType.DMA((blocks, pieces)),
            pltpu.SemaphoreType.DMA((blocks, pieces)),
            pltpu.SemaphoreType.DMA((2,)),
            pltpu.SemaphoreType.DMA((2,)),
            pltpu.SemaphoreType.REGULAR((4,)),
        ],
        compiler_params=pltpu.CompilerParams(
            collective_id=0, has_side_effects=True, vmem_limit_bytes=56 * 1024 * 1024
        ),
        cost_estimate=pl.CostEstimate(
            flops=10 * wide * blocks * tok * HD,
            bytes_accessed=2 * 3 * tok * q_cols,
            transcendentals=wide * blocks * tok,
        ),
    )(doc_lengths, queries, keys, values, out_grad)
    return dq, dk, dv, rms[0, 0]


def solution(mesh):
    sizes = (mesh.shape["ctx"], mesh.shape["head"])
    return jax.shard_map(
        partial(local, sizes),
        mesh=mesh,
        in_specs=(P("ctx", "head"), P("ctx", "head"), P("ctx", "head"), P("ctx", "head"), P()),
        out_specs=(P("ctx", "head"), P("ctx", "head"), P("ctx", "head"), P()),
        check_vma=False,
    )
```
